512 devices in a mesh: vec: 16 (over x, z_hi, core), lat: 32 (over z_lo, y).
Axes of the slice: x: 4, y: 4, z: 16 (z_hi: 2, z_lo: 8; z = z_hi * 8 + z_lo), core: 2. Of those that a mesh axis runs over, the one named last changes fastest.
Arguments:
- perturbation: float32 [128, 3, 256, 2048], P('vec', None, 'lat'), may hold values from -6 to 6
- wind_coriolis: float32 [4, 3, 256, 2048], P(None, None, 'lat', 'vec'), may hold values from -4 to 4
- depth_field: float32 [4, 256, 2048], P(None, 'lat', 'vec'), may hold values from 0.5 to 2
Outputs:
- evolved: float32 [128, 3, 256, 2048], P('vec', None, 'lat')
The draws below stay inside these ranges and needn't reach their ends.
All inputs are finite; a program needn't handle non-finite values.
Results may differ from the reference program's by a relative error of at most 0.00002.
Values sent between devices are 32-bit elements; how exact they have to be, the bound alone decides.
No kernel may reach another device: no remote copies, remote signals or barrier semaphores. Data moves between devices by JAX's collectives and lax.ppermute only.
A program may use at most 64 MiB of HBM per device.

```python
import math
import jax
import jax.numpy as jnp
from jax import lax

NLON = 2048
STEPS = 4
VECTORS = 128
NLAT = 256


def steps_of(rng, extent, split, smallest, top_value):
    def one(dim, blocks):
        steps = jax.random.uniform(jax.random.fold_in(jax.random.fold_in(rng, 6), dim), (blocks,), jnp.float32, smallest / len(split), top_value / len(split))
        return jnp.repeat(jnp.exp(steps), extent[dim] // blocks).reshape((-1,) + (1,) * (len(extent) - dim - 1))

    loudness = one(*split[0])
    for cut in split[1:]:
        loudness = loudness * one(*cut)
    return loudness


def scatter_about(key, extent, width, most, split=(), kind=jnp.bfloat16):
    values = jax.random.normal(key, extent, jnp.float32) * width
    if len(split) > 0:
        values = steps_of(key, extent, split, -0.22, 0.18) * values
    return jnp.clip(values, min=-most, max=most).astype(kind)


def setup_inputs(seed: int = 0) -> dict:
    streams_of = jax.random.split(jax.random.key(seed), 4)
    return {
        "perturbation": scatter_about(streams_of[0], (VECTORS, 3, NLAT, NLON), 1.0, 6.0, ((0, 16), (2, 32)), jnp.float32),
        "wind_coriolis": scatter_about(streams_of[1], (STEPS, 3, NLAT, NLON), 1.0, 4.0, ((2, 32), (3, 16)), jnp.float32),
        "depth_field": jnp.clip(jnp.exp(math.log(2.0) - 1.3862944 * jax.random.uniform(streams_of[2], (STEPS, NLAT, NLON), jnp.float32) ** steps_of(streams_of[2], (STEPS, NLAT, NLON), ((1, 32), (2, 16)), -0.2, 0.2)), 0.5, 2.0),
    }


time_step = 0.2
viscosity = 0.05


def lon_diff(field):
    return 0.5 * (jnp.roll(field, -1, axis=-1) - jnp.roll(field, 1, axis=-1))


def lat_diff(padded):
    return 0.5 * (padded[..., 2:, :] - padded[..., :-2, :])


def smooth(padded, centre):
    return padded[..., 2:, :] + padded[..., :-2, :] + jnp.roll(centre, -1, axis=-1) + jnp.roll(centre, 1, axis=-1) - 4.0 * centre


def advance(padded, coefficients):
    height_pad = padded[..., 0, :, :]
    zonal_pad = padded[..., 1, :, :]
    north_pad = padded[..., 2, :, :]
    height = height_pad[..., 1:-1, :]
    zonal = zonal_pad[..., 1:-1, :]
    north = north_pad[..., 1:-1, :]
    east_wind = coefficients[0]
    north_wind = coefficients[1]
    rotation = coefficients[2]
    depth_now = coefficients[3]
    tend_height = -(east_wind * lon_diff(height) + north_wind * lat_diff(height_pad) + depth_now * (lon_diff(zonal) + lat_diff(north_pad)))
    tend_zonal = -(east_wind * lon_diff(zonal) + north_wind * lat_diff(zonal_pad)) + rotation * north - lon_diff(height)
    tend_north = -(east_wind * lon_diff(north) + north_wind * lat_diff(north_pad)) - rotation * zonal - lat_diff(height_pad)
    new_height = height + time_step * (tend_height + viscosity * smooth(height_pad, height))
    new_zonal = zonal + time_step * (tend_zonal + viscosity * smooth(zonal_pad, zonal))
    new_north = north + time_step * (tend_north + viscosity * smooth(north_pad, north))
    return jnp.stack([new_height, new_zonal, new_north], axis=-3)


def reference(perturbation, wind_coriolis, depth_field):
    coefficients = jnp.concatenate([wind_coriolis, depth_field[:, None]], axis=1)

    def single(state):
        for moment in range(STEPS):
            padded = jnp.pad(state, ((0, 0), (1, 1), (0, 0)))
            state = advance(padded, coefficients[moment])
        return state

    return lax.map(single, perturbation)
```

```python
import jax
import jax.numpy as jnp
from jax import lax
from jax.experimental import pallas as pl
from jax.experimental.pallas import tpu as pltpu
from jax.sharding import Mesh, PartitionSpec as P

STEPS = 4
HALO = 4
LANES = 128

time_step = 0.2
viscosity = 0.05

KEEP = 1.0 - 4.0 * time_step * viscosity
SPREAD = time_step * viscosity / KEEP
SLOPE = time_step / (2.0 * KEEP)
HEIGHT = 2.0 * KEEP / time_step

VMEM = pl.BlockSpec(memory_space=pltpu.VMEM)
SMEM = pl.BlockSpec(memory_space=pltpu.SMEM)


def split_rows(state_ref, low_ref, high_ref):
    fields, rows, lon = state_ref.shape[1:]
    half = rows // 2

    for field in range(fields):

        @pl.loop(0, lon // LANES)
        def _(tile):
            lanes = pl.ds(pl.multiple_of(tile * LANES, LANES), LANES)
            block = jnp.swapaxes(state_ref[:, field, :, lanes], 0, 1)
            if field == 0:
                block = block * (1.0 / HEIGHT)
            low_ref[field, :, :, lanes] = block[:half]
            high_ref[field, :, :, lanes] = block[half:]


def rows_first(state):
    vectors, fields, rows, lon = state.shape
    half = jax.ShapeDtypeStruct((fields, rows // 2, vectors, lon), state.dtype)
    return pl.pallas_call(
        split_rows,
        out_shape=(half, half),
        in_specs=[VMEM],
        out_specs=(VMEM, VMEM),
        compiler_params=pltpu.CompilerParams(vmem_limit_bytes=40 << 20),
    )(state)


def step_row(source, target, plus, minus, raw, moment, row, crow, tiles, edge):
    def at(field, r, tile):
        return source[field, r, :, pl.ds(tile * LANES, LANES)]

    first_lane, last_lane = edge
    held = {}

    def turned(field, tile):
        tile %= tiles
        if (field, tile) not in held:
            value = at(field, row, tile)
            held[field, tile] = (
                value,
                pltpu.roll(value, 1, 1),
                pltpu.roll(value, LANES - 1, 1),
            )
        return held[field, tile]

    def coefficient(ref, tile, channel):
        line = ref[tile, crow, pl.ds(moment * 4 + channel, 1), :]
        return jnp.broadcast_to(line, (8, LANES))

    for tile in range(tiles):
        middle, west, east, south, north = ([], [], [], [], [])
        for field in range(3):
            value, right, left = turned(field, tile)
            middle.append(value)
            west.append(jnp.where(first_lane, turned(field, tile - 1)[1], right))
            east.append(jnp.where(last_lane, turned(field, tile + 1)[2], left))
            south.append(at(field, row - 1, tile))
            north.append(at(field, row + 1, tile))
        to_east = coefficient(plus, tile, 0)
        to_west = coefficient(minus, tile, 0)
        to_north = coefficient(plus, tile, 1)
        to_south = coefficient(minus, tile, 1)
        turn = coefficient(raw, tile, 2)
        depth = coefficient(raw, tile, 3)
        new = [
            (middle[f] + to_east * east[f])
            + (to_west * west[f] + to_north * north[f])
            + to_south * south[f]
            for f in range(3)
        ]
        new[0] = new[0] + depth * ((east[1] - west[1]) + (north[2] - south[2]))
        new[1] = new[1] + (turn * middle[2] - (east[0] - west[0]))
        new[2] = new[2] - (turn * middle[1] + (north[0] - south[0]))
        for field in range(3):
            target(field, tile, new[field])


def advance_all(
    lat_ref, low_ref, high_ref, below_ref, above_ref, own_ref, cbelow_ref, cabove_ref,
    out_ref, first, second, last, raw, plus, minus, sems
):
    tiles = raw.shape[0]
    rows = out_ref.shape[2]
    half = rows // 2
    copies = [
        pltpu.make_async_copy(ref, first.at[:, pl.ds(start, count)], sems.at[k])
        for k, (ref, start, count) in enumerate(
            [
                (below_ref, 0, HALO),
                (low_ref, HALO, half),
                (high_ref, HALO + half, half),
                (above_ref, HALO + rows, HALO),
            ]
        )
    ]
    for copy in copies:
        copy.start()

    second[:, HALO - 1] = jnp.zeros_like(second[:, HALO - 1])
    second[:, HALO + rows] = jnp.zeros_like(second[:, HALO + rows])

    @pl.loop(0, tiles)
    def _(tile):
        def put(row, group, value):
            lines = pl.ds(group * 8, 8)
            raw[tile, row, lines, :] = value
            plus[tile, row, lines, :] = SPREAD + value
            minus[tile, row, lines, :] = SPREAD - value

        core, rest = (tile % 2, tile // 2)
        for row in range(rows):
            for group in range(2):
                put(3 + row, group, own_ref[core, rest, row, pl.ds(group * 8, 8), :])
        for place, (row, group) in enumerate([(0, 0), (1, 0), (2, 0), (2, 1)]):
            put(row, group, cbelow_ref[core, rest, place])
        for place, (row, group) in enumerate([(13, 0), (12, 0), (11, 0), (11, 1)]):
            put(row, group, cabove_ref[core, rest, place])

    for copy in copies:
        copy.wait()

    lane = lax.broadcasted_iota(jnp.int32, (8, LANES), 1)
    edge = (lane == 0, lane == LANES - 1)
    buffers = [first, second]
    for moment in range(STEPS):
        source, goal = (buffers[moment % 2], buffers[(moment + 1) % 2])
        final = moment == STEPS - 1
        start = jnp.where(lat_ref[0] == 0, HALO, moment + 1)
        stop = jnp.where(lat_ref[0] == lat_ref[1] - 1, HALO + rows, HALO + rows + 3 - moment)

        @pl.loop(start, stop)
        def _(row):
            def target(field, tile, value):
                lanes = pl.ds(tile * LANES, LANES)
                if final:
                    scale = KEEP**STEPS * (HEIGHT if field == 0 else 1.0)
                    last[field, row - HALO, :, lanes] = value * scale
                else:
                    goal[field, row, :, lanes] = value

            step_row(source, target, plus, minus, raw, moment, row, row - 1, tiles, edge)

    for field in range(3):

        @pl.loop(0, tiles)
        def _(tile):
            lanes = pl.ds(pl.multiple_of(tile * LANES, LANES), LANES)
            out_ref[:, field, :, lanes] = jnp.swapaxes(last[field, :, :, lanes], 0, 1)


def shards(perturbation, wind_coriolis, depth_field):
    vectors, fields, rows, lon = perturbation.shape
    tiles = lon // LANES
    count = lax.axis_size("lat")
    up = [(i, i + 1) for i in range(count - 1)]
    down = [(i + 1, i) for i in range(count - 1)]

    low, high = rows_first(perturbation)
    below = lax.ppermute(high, "lat", up)
    above = lax.ppermute(low, "lat", down)

    scales = jnp.array([-SLOPE, -SLOPE, 2.0 * SLOPE], jnp.float32)[None, :, None, None]
    packed = jnp.concatenate([wind_coriolis * scales, -SLOPE * SLOPE * depth_field[:, None]], axis=1)
    packed = packed.transpose(2, 0, 1, 3).reshape(rows, STEPS * 4, LANES)
    gathered = lax.all_gather(packed, "zh", axis=0)
    gathered = lax.all_gather(gathered, "x", axis=0)
    gathered = gathered.reshape(tiles // 2, rows, STEPS * 4, LANES)
    gathered = lax.all_gather(gathered, "core", axis=0)

    def picked(order):
        return jnp.stack([gathered[:, :, row, group * 8 : group * 8 + 8] for row, group in order], axis=2)

    cbelow = lax.ppermute(picked([(5, 0), (6, 0), (7, 0), (7, 1)]), "lat", up)
    cabove = lax.ppermute(picked([(2, 0), (1, 0), (0, 0), (0, 1)]), "lat", down)

    where = jnp.stack([lax.axis_index("lat"), jnp.int32(count)]).astype(jnp.int32)
    anywhere = pl.BlockSpec(memory_space=pl.ANY)
    table = pltpu.VMEM((tiles, rows + 6, STEPS * 4, LANES), jnp.float32)
    band = pltpu.VMEM((fields, rows + 2 * HALO, vectors, lon), jnp.float32)
    return pl.pallas_call(
        advance_all,
        out_shape=jax.ShapeDtypeStruct(perturbation.shape, perturbation.dtype),
        in_specs=[SMEM] + [anywhere] * 4 + [VMEM] * 3,
        out_specs=VMEM,
        scratch_shapes=[
            band,
            band,
            pltpu.VMEM((fields, rows, vectors, lon), jnp.float32),
            table,
            table,
            table,
            pltpu.SemaphoreType.DMA((4,)),
        ],
        compiler_params=pltpu.CompilerParams(vmem_limit_bytes=40 << 20),
    )(where, low, high, below, above, gathered, cbelow, cabove)


def solution(mesh):
    grid = Mesh(
        mesh.devices.reshape(mesh.shape["vec"] // 4, 2, 2, mesh.shape["lat"]), ("x", "zh", "core", "lat")
    )
    vec = ("x", "zh", "core")
    placed = (P(vec, None, "lat", None), P(None, None, "lat", vec), P(None, "lat", vec))
    return jax.shard_map(
        shards, mesh=grid, in_specs=placed, out_specs=P(vec, None, "lat", None), check_vma=False
    )
```

```python
import jax
import jax.numpy as jnp
from jax import lax
from jax.experimental import pallas as pl
from jax.experimental.pallas import tpu as pltpu
from jax.sharding import Mesh, PartitionSpec as P

STEPS = 4
HALO = 4
LANES = 128

time_step = 0.2
viscosity = 0.05

KEEP = 1.0 - 4.0 * time_step * viscosity
SPREAD = time_step * viscosity / KEEP
SLOPE = time_step / (2.0 * KEEP)
HEIGHT = 2.0 * KEEP / time_step

VMEM = pl.BlockSpec(memory_space=pltpu.VMEM)
SMEM = pl.BlockSpec(memory_space=pltpu.SMEM)


def room(mebibytes):
    return pltpu.CompilerParams(vmem_limit_bytes=mebibytes << 20)


def split_rows(state_ref, low_ref, high_ref):
    fields, rows, lon = state_ref.shape[1:]
    half = rows // 2

    for field in range(fields):

        @pl.loop(0, lon // LANES)
        def _(tile):
            lanes = pl.ds(pl.multiple_of(tile * LANES, LANES), LANES)
            block = jnp.swapaxes(state_ref[:, field, :, lanes], 0, 1)
            if field == 0:
                block = block * (1.0 / HEIGHT)
            low_ref[field, :, :, lanes] = block[:half]
            high_ref[field, :, :, lanes] = block[half:]


def rows_first(state):
    vectors, fields, rows, lon = state.shape
    half = jax.ShapeDtypeStruct((fields, rows // 2, vectors, lon), state.dtype)
    return pl.pallas_call(
        split_rows,
        out_shape=(half, half),
        in_specs=[VMEM],
        out_specs=(VMEM, VMEM),
        compiler_params=room(8),
    )(state)


def pack(wind_ref, depth_ref, out_ref):
    for pair in range(STEPS // 2):
        planes = []
        for moment in (2 * pair, 2 * pair + 1):
            planes += [wind_ref[moment, 0] * -SLOPE, wind_ref[moment, 1] * -SLOPE]
            planes += [wind_ref[moment, 2] * (2.0 * SLOPE), depth_ref[moment] * (-SLOPE * SLOPE)]
        out_ref[:, pl.ds(8 * pair, 8), :] = jnp.swapaxes(jnp.stack(planes), 0, 1)


def pick_halo(mine_ref, other_ref, up_ref, down_ref):
    for core, gathered in enumerate((mine_ref, other_ref)):

        @pl.loop(0, gathered.shape[0])
        def _(quad):
            for side in range(2):
                for out, far, mid, near in ((up_ref, 5, 6, 7), (down_ref, 2, 1, 0)):
                    out[core, quad, side, 0] = gathered[quad, side, mid, :8]
                    out[core, quad, side, 1] = gathered[quad, side, near, :8]
                    out[core, quad, side, 2, :4] = gathered[quad, side, far, :4]
                    out[core, quad, side, 2, 4:] = gathered[quad, side, near, 8:12]


def step_row(source, target, plus, minus, raw, moment, row, crow, tiles, edge):
    def at(field, r, tile):
        return source[field, r, :, pl.ds(tile * LANES, LANES)]

    first_lane, last_lane = edge
    held = {}

    def turned(field, tile):
        tile %= tiles
        if (field, tile) not in held:
            value = at(field, row, tile)
            held[field, tile] = (
                value,
                pltpu.roll(value, 1, 1),
                pltpu.roll(value, LANES - 1, 1),
            )
        return held[field, tile]

    def coefficient(ref, tile, channel):
        line = ref[tile, crow, pl.ds(moment * 4 + channel, 1), :]
        return jnp.broadcast_to(line, (8, LANES))

    for tile in range(tiles):
        middle, west, east, south, north = ([], [], [], [], [])
        for field in range(3):
            value, right, left = turned(field, tile)
            middle.append(value)
            west.append(jnp.where(first_lane, turned(field, tile - 1)[1], right))
            east.append(jnp.where(last_lane, turned(field, tile + 1)[2], left))
            south.append(at(field, row - 1, tile))
            north.append(at(field, row + 1, tile))
        to_east = coefficient(plus, tile, 0)
        to_west = coefficient(minus, tile, 0)
        to_north = coefficient(plus, tile, 1)
        to_south = coefficient(minus, tile, 1)
        turn = coefficient(raw, tile, 2)
        depth = coefficient(raw, tile, 3)
        new = [
            (middle[f] + to_east * east[f])
            + (to_west * west[f] + to_north * north[f])
            + to_south * south[f]
            for f in range(3)
        ]
        new[0] = new[0] + depth * ((east[1] - west[1]) + (north[2] - south[2]))
        new[1] = new[1] + (turn * middle[2] - (east[0] - west[0]))
        new[2] = new[2] - (turn * middle[1] + (north[0] - south[0]))
        for field in range(3):
            target(field, row, tile, new[field])


def advance_all(
    place_ref, low_ref, high_ref, below_ref, above_ref, mine_ref, other_ref, cbelow_ref, cabove_ref,
    out_ref, first, second, last, raw, plus, minus, sems
):
    tiles = raw.shape[0]
    rows = out_ref.shape[2]
    half = rows // 2
    copies = [
        pltpu.make_async_copy(ref, first.at[:, pl.ds(start, count)], sems.at[k])
        for k, (ref, start, count) in enumerate(
            [
                (below_ref, 0, HALO),
                (low_ref, HALO, half),
                (high_ref, HALO + half, half),
                (above_ref, HALO + rows, HALO),
            ]
        )
    ]
    for copy in copies:
        copy.start()

    @pl.loop(0, tiles // 4)
    def _(quad):
        for core, gathered in enumerate((mine_ref, other_ref)):
            for side in range(2):
                tile = quad * 4 + (side ^ place_ref[2]) * 2 + (core ^ place_ref[3])

                def put(row, line, value):
                    lines = pl.ds(line, value.shape[0])
                    raw[tile, row, lines, :] = value
                    plus[tile, row, lines, :] = SPREAD + value
                    minus[tile, row, lines, :] = SPREAD - value

                for row in range(rows):
                    for line in (0, 8):
                        put(3 + row, line, gathered[quad, side, row, pl.ds(line, 8), :])
                for halo, far, mid, near in ((cbelow_ref, 0, 1, 2), (cabove_ref, 13, 12, 11)):
                    put(mid, 0, halo[core, quad, side, 0])
                    put(near, 0, halo[core, quad, side, 1])
                    put(far, 0, halo[core, quad, side, 2, :4])
                    put(near, 8, halo[core, quad, side, 2, 4:])

    for copy in copies:
        copy.wait()

    lane = lax.broadcasted_iota(jnp.int32, (8, LANES), 1)
    edge = (lane == 0, lane == LANES - 1)
    buffers = [first, second]
    for moment in range(STEPS):
        source, goal = (buffers[moment % 2], buffers[(moment + 1) % 2])
        final = moment == STEPS - 1

        @pl.loop(moment + 1, HALO + rows + 3 - moment, step=2)
        def _(pair):
            def target(field, row, tile, value):
                lanes = pl.ds(tile * LANES, LANES)
                if final:
                    scale = KEEP**STEPS * (HEIGHT if field == 0 else 1.0)
                    last[field, row - HALO, :, lanes] = value * scale
                else:
                    goal[field, row, :, lanes] = value

            for row in (pair, pair + 1):
                step_row(source, target, plus, minus, raw, moment, row, row - 1, tiles, edge)

        if not final:

            @pl.when(place_ref[0] == 0)
            def _():
                goal[:, HALO - 1] = jnp.zeros_like(goal[:, HALO - 1])

            @pl.when(place_ref[0] == place_ref[1] - 1)
            def _():
                goal[:, HALO + rows] = jnp.zeros_like(goal[:, HALO + rows])

    for field in range(3):

        @pl.loop(0, tiles)
        def _(tile):
            lanes = pl.ds(pl.multiple_of(tile * LANES, LANES), LANES)
            out_ref[:, field, :, lanes] = jnp.swapaxes(last[field, :, :, lanes], 0, 1)


def shards(perturbation, wind_coriolis, depth_field):
    vectors, fields, rows, lon = perturbation.shape
    tiles = lon // LANES
    count = lax.axis_size("lat")
    up = [(i, i + 1) for i in range(count - 1)]
    down = [(i + 1, i) for i in range(count - 1)]

    low, high = rows_first(perturbation)
    below = lax.ppermute(high, "lat", up)
    above = lax.ppermute(low, "lat", down)

    packed = pl.pallas_call(
        pack,
        out_shape=jax.ShapeDtypeStruct((rows, STEPS * 4, LANES), jnp.float32),
        in_specs=[VMEM] * 2,
        out_specs=VMEM,
        compiler_params=room(4),
    )(wind_coriolis, depth_field)
    swap = [(0, 1), (1, 0)]
    mine = jnp.stack([packed, lax.ppermute(packed, "zh", swap)])
    mine = lax.all_gather(mine, "x", axis=0)
    other = lax.ppermute(mine, "core", swap)
    picked = jax.ShapeDtypeStruct((2, tiles // 4, 2, 3, 8, LANES), jnp.float32)
    to_up, to_down = pl.pallas_call(
        pick_halo,
        out_shape=(picked, picked),
        in_specs=[VMEM] * 2,
        out_specs=(VMEM, VMEM),
        compiler_params=room(4),
    )(mine, other)
    cbelow = lax.ppermute(to_up, "lat", up)
    cabove = lax.ppermute(to_down, "lat", down)

    place = [lax.axis_index("lat"), count, lax.axis_index("zh"), lax.axis_index("core")]
    place = jnp.stack([jnp.int32(number) for number in place])
    anywhere = pl.BlockSpec(memory_space=pl.ANY)
    table = pltpu.VMEM((tiles, rows + 6, STEPS * 4, LANES), jnp.float32)
    band = pltpu.VMEM((fields, rows + 2 * HALO, vectors, lon), jnp.float32)
    return pl.pallas_call(
        advance_all,
        out_shape=jax.ShapeDtypeStruct(perturbation.shape, perturbation.dtype),
        in_specs=[SMEM] + [anywhere] * 4 + [VMEM] * 4,
        out_specs=VMEM,
        scratch_shapes=[
            band,
            band,
            pltpu.VMEM((fields, rows, vectors, lon), jnp.float32),
            table,
            table,
            table,
            pltpu.SemaphoreType.DMA((4,)),
        ],
        compiler_params=room(24),
    )(place, low, high, below, above, mine, other, cbelow, cabove)


def solution(mesh):
    grid = Mesh(
        mesh.devices.reshape(mesh.shape["vec"] // 4, 2, 2, mesh.shape["lat"]), ("x", "zh", "core", "lat")
    )
    vec = ("x", "zh", "core")
    placed = (P(vec, None, "lat", None), P(None, None, "lat", vec), P(None, "lat", vec))
    return jax.shard_map(
        shards, mesh=grid, in_specs=placed, out_specs=P(vec, None, "lat", None), check_vma=False
    )
```

```python
import jax
import jax.numpy as jnp
from jax import lax
from jax.experimental import pallas as pl
from jax.experimental.pallas import tpu as pltpu
from jax.sharding import Mesh, PartitionSpec as P

STEPS = 4
HALO = 4
UNROLL = 2
LANES = 128

time_step = 0.2
viscosity = 0.05

KEEP = 1.0 - 4.0 * time_step * viscosity
SPREAD = time_step * viscosity / KEEP
SLOPE = time_step / (2.0 * KEEP)
HEIGHT = 2.0 * KEEP / time_step

VMEM = pl.BlockSpec(memory_space=pltpu.VMEM)
SMEM = pl.BlockSpec(memory_space=pltpu.SMEM)


def room(mebibytes):
    return pltpu.CompilerParams(vmem_limit_bytes=mebibytes << 20)


def split_rows(state_ref, low_ref, high_ref):
    fields, rows, lon = state_ref.shape[1:]
    half = rows // 2

    for field in range(fields):

        @pl.loop(0, lon // LANES)
        def _(tile):
            lanes = pl.ds(pl.multiple_of(tile * LANES, LANES), LANES)
            block = jnp.swapaxes(state_ref[:, field, :, lanes], 0, 1)
            if field == 0:
                block = block * (1.0 / HEIGHT)
            low_ref[field, :, :, lanes] = block[:half]
            high_ref[field, :, :, lanes] = block[half:]


def rows_first(state):
    vectors, fields, rows, lon = state.shape
    half = jax.ShapeDtypeStruct((fields, rows // 2, vectors, lon), state.dtype)
    return pl.pallas_call(
        split_rows,
        out_shape=(half, half),
        in_specs=[VMEM],
        out_specs=(VMEM, VMEM),
        compiler_params=room(8),
    )(state)


def pack(wind_ref, depth_ref, own_ref, up_ref, down_ref):
    for pair in range(STEPS // 2):
        planes = []
        for moment in (2 * pair, 2 * pair + 1):
            planes += [wind_ref[moment, 0] * -SLOPE, wind_ref[moment, 1] * -SLOPE]
            planes += [wind_ref[moment, 2] * (2.0 * SLOPE), depth_ref[moment] * (-SLOPE * SLOPE)]
        block = jnp.swapaxes(jnp.stack(planes), 0, 1)
        for row in range(block.shape[0]):
            own_ref[2 * row + pair] = block[row]
        for out, far, mid, near in ((up_ref, 5, 6, 7), (down_ref, 2, 1, 0)):
            if pair == 0:
                out[0] = block[mid]
                out[1] = block[near]
                out[2, :4] = block[far, :4]
            else:
                out[2, 4:] = block[near, :4]


def step_row(source, target, plus, minus, raw, moment, row, crow, tiles, edge):
    def at(field, r, tile):
        return source[field, r, :, pl.ds(tile * LANES, LANES)]

    first_lane, last_lane = edge
    held = {}

    def turned(field, tile):
        tile %= tiles
        if (field, tile) not in held:
            value = at(field, row, tile)
            held[field, tile] = (
                value,
                pltpu.roll(value, 1, 1),
                pltpu.roll(value, LANES - 1, 1),
            )
        return held[field, tile]

    def coefficient(ref, tile, channel):
        line = ref[tile, crow, pl.ds(moment * 4 + channel, 1), :]
        return jnp.broadcast_to(line, (8, LANES))

    for tile in range(tiles):
        middle, west, east, south, north = ([], [], [], [], [])
        for field in range(3):
            value, right, left = turned(field, tile)
            middle.append(value)
            west.append(jnp.where(first_lane, turned(field, tile - 1)[1], right))
            east.append(jnp.where(last_lane, turned(field, tile + 1)[2], left))
            south.append(at(field, row - 1, tile))
            north.append(at(field, row + 1, tile))
        to_east = coefficient(plus, tile, 0)
        to_west = coefficient(minus, tile, 0)
        to_north = coefficient(plus, tile, 1)
        to_south = coefficient(minus, tile, 1)
        turn = coefficient(raw, tile, 2)
        depth = coefficient(raw, tile, 3)
        new = [
            (middle[f] + to_east * east[f])
            + (to_west * west[f] + to_north * north[f])
            + to_south * south[f]
            for f in range(3)
        ]
        new[0] = new[0] + depth * ((east[1] - west[1]) + (north[2] - south[2]))
        new[1] = new[1] + (turn * middle[2] - (east[0] - west[0]))
        new[2] = new[2] - (turn * middle[1] + (north[0] - south[0]))
        for field in range(3):
            target(field, row, tile, new[field])


def lay_band(below_ref, low_ref, high_ref, above_ref, band_ref):
    for field in range(band_ref.shape[0]):
        start = 0
        for ref in (below_ref, low_ref, high_ref, above_ref):
            for row in range(ref.shape[1]):
                band_ref[field, start + row] = ref[field, row]
            start += ref.shape[1]


def advance_all(
    place_ref, band_ref, mine_ref, other_ref, out_ref, first, second, last, raw, plus, minus, sems
):
    tiles = raw.shape[0]
    rows = out_ref.shape[2]

    @pl.loop(0, tiles // 4)
    def _(quad):
        for core, gathered in enumerate((mine_ref, other_ref)):
            for side in range(2):
                tile = quad * 4 + (side ^ place_ref[2]) * 2 + (core ^ place_ref[3])

                def put(row, line, value):
                    lines = pl.ds(line, value.shape[0])
                    raw[tile, row, lines, :] = value
                    plus[tile, row, lines, :] = SPREAD + value
                    minus[tile, row, lines, :] = SPREAD - value

                for row in range(rows):
                    for pair in range(2):
                        put(3 + row, 8 * pair, gathered[quad, side, 2 * row + pair])
                for start, far, mid, near in ((2 * rows, 0, 1, 2), (2 * rows + 3, 13, 12, 11)):
                    put(mid, 0, gathered[quad, side, start])
                    put(near, 0, gathered[quad, side, start + 1])
                    put(far, 0, gathered[quad, side, start + 2, :4])
                    put(near, 8, gathered[quad, side, start + 2, 4:])

    lane = lax.broadcasted_iota(jnp.int32, (8, LANES), 1)
    edge = (lane == 0, lane == LANES - 1)

    def leaving(field, row):
        return pltpu.make_async_copy(last.at[field, row], out_ref.at[:, field, row], sems.at[field, row])

    for moment, (source, goal) in enumerate([(band_ref, first), (first, second), (second, first), (first, last)]):
        final = moment == STEPS - 1

        def rows_of(start, count):
            def target(field, row, tile, value):
                lanes = pl.ds(tile * LANES, LANES)
                if final:
                    scale = KEEP**STEPS * (HEIGHT if field == 0 else 1.0)
                    goal[field, row - HALO, :, lanes] = value * scale
                else:
                    goal[field, row, :, lanes] = value

            for row in range(count):
                row += start
                step_row(source, target, plus, minus, raw, moment, row, row - 1, tiles, edge)
                if final:
                    for field in range(3):
                        leaving(field, row - HALO).start()

        begin, count = (moment + 1, rows + 2 * (STEPS - 1 - moment))

        @pl.loop(begin, begin + count, step=UNROLL)
        def _(row):
            rows_of(row, UNROLL)

        if not final:

            @pl.when(place_ref[0] == 0)
            def _():
                goal[:, HALO - 1] = jnp.zeros_like(goal[:, HALO - 1])

            @pl.when(place_ref[0] == place_ref[1] - 1)
            def _():
                goal[:, HALO + rows] = jnp.zeros_like(goal[:, HALO + rows])

    @pl.loop(0, rows)
    def _(row):
        for field in range(3):
            leaving(field, row).wait()


def shards(perturbation, wind_coriolis, depth_field):
    vectors, fields, rows, lon = perturbation.shape
    tiles = lon // LANES
    count = lax.axis_size("lat")
    up = [(i, i + 1) for i in range(count - 1)]
    down = [(i + 1, i) for i in range(count - 1)]

    low, high = rows_first(perturbation)
    below = lax.ppermute(high, "lat", up)
    above = lax.ppermute(low, "lat", down)

    few = jax.ShapeDtypeStruct((3, 8, LANES), jnp.float32)
    own, to_up, to_down = pl.pallas_call(
        pack,
        out_shape=(jax.ShapeDtypeStruct((2 * rows, 8, LANES), jnp.float32), few, few),
        in_specs=[VMEM] * 2,
        out_specs=(VMEM,) * 3,
        compiler_params=room(4),
    )(wind_coriolis, depth_field)
    own = jnp.concatenate([own, lax.ppermute(to_up, "lat", up), lax.ppermute(to_down, "lat", down)])
    own, low, high = lax.optimization_barrier((own, low, high))
    swap = [(0, 1), (1, 0)]
    mine = jnp.stack([own, lax.ppermute(own, "zh", swap)])
    mine = lax.all_gather(mine, "x", axis=0)
    other = lax.ppermute(mine, "core", swap)

    place = [lax.axis_index("lat"), count, lax.axis_index("zh"), lax.axis_index("core")]
    place = jnp.stack([jnp.int32(number) for number in place])
    table = pltpu.VMEM((tiles, rows + 6, STEPS * 4, LANES), jnp.float32)
    band = (fields, rows + 2 * HALO, vectors, lon)
    laid = pl.pallas_call(
        lay_band,
        out_shape=jax.ShapeDtypeStruct(band, jnp.float32),
        in_specs=[VMEM] * 4,
        out_specs=VMEM,
        compiler_params=room(8),
    )(below, low, high, above)
    return pl.pallas_call(
        advance_all,
        out_shape=jax.ShapeDtypeStruct(perturbation.shape, perturbation.dtype),
        in_specs=[SMEM] + [VMEM] * 3,
        out_specs=pl.BlockSpec(memory_space=pl.ANY),
        scratch_shapes=[
            pltpu.VMEM(band, jnp.float32),
            pltpu.VMEM(band, jnp.float32),
            pltpu.VMEM((fields, rows, vectors, lon), jnp.float32),
            table,
            table,
            table,
            pltpu.SemaphoreType.DMA((fields, rows)),
        ],
        compiler_params=room(14),
    )(place, laid, mine, other)


def solution(mesh):
    grid = Mesh(
        mesh.devices.reshape(mesh.shape["vec"] // 4, 2, 2, mesh.shape["lat"]), ("x", "zh", "core", "lat")
    )
    vec = ("x", "zh", "core")
    placed = (P(vec, None, "lat", None), P(None, None, "lat", vec), P(None, "lat", vec))
    return jax.shard_map(
        shards, mesh=grid, in_specs=placed, out_specs=P(vec, None, "lat", None), check_vma=False
    )
```

```python
import jax
import jax.numpy as jnp
from jax import lax
from jax.experimental import pallas as pl
from jax.experimental.pallas import tpu as pltpu
from jax.sharding import Mesh, PartitionSpec as P

STEPS = 4
HALO = 4
BLOCK = 4
LANES = 128

time_step = 0.2
viscosity = 0.05

KEEP = 1.0 - 4.0 * time_step * viscosity
SPREAD = time_step * viscosity / KEEP
SLOPE = time_step / (2.0 * KEEP)
HEIGHT = 2.0 * KEEP / time_step

VMEM = pl.BlockSpec(memory_space=pltpu.VMEM)
HBM = pl.BlockSpec(memory_space=pl.ANY)
SMEM = pl.BlockSpec(memory_space=pltpu.SMEM)


def room(mebibytes):
    return pltpu.CompilerParams(vmem_limit_bytes=mebibytes << 20)


def split_rows(state_ref, low_ref, high_ref):
    fields, rows, lon = state_ref.shape[1:]
    half = rows // 2

    for field in range(fields):

        @pl.loop(0, lon // LANES)
        def _(tile):
            lanes = pl.ds(pl.multiple_of(tile * LANES, LANES), LANES)
            block = jnp.swapaxes(state_ref[:, field, :, lanes], 0, 1)
            if field == 0:
                block = block * (1.0 / HEIGHT)
            low_ref[field, :, :, lanes] = block[:half]
            high_ref[field, :, :, lanes] = block[half:]


def rows_first(state):
    vectors, fields, rows, lon = state.shape
    half = jax.ShapeDtypeStruct((fields, rows // 2, vectors, lon), state.dtype)
    return pl.pallas_call(
        split_rows,
        out_shape=(half, half),
        in_specs=[VMEM],
        out_specs=(VMEM, VMEM),
        compiler_params=room(8),
    )(state)


def pack(wind_ref, depth_ref, own_ref, up_ref, down_ref):
    for pair in range(STEPS // 2):
        planes = []
        for moment in (2 * pair, 2 * pair + 1):
            planes += [wind_ref[moment, 0] * -SLOPE, wind_ref[moment, 1] * -SLOPE]
            planes += [wind_ref[moment, 2] * (2.0 * SLOPE), depth_ref[moment] * (-SLOPE * SLOPE)]
        block = jnp.swapaxes(jnp.stack(planes), 0, 1)
        for row in range(block.shape[0]):
            own_ref[2 * row + pair] = block[row]
        for out, far, mid, near in ((up_ref, 5, 6, 7), (down_ref, 2, 1, 0)):
            if pair == 0:
                out[0] = block[mid]
                out[1] = block[near]
                out[2, :4] = block[far, :4]
            else:
                out[2, 4:] = block[near, :4]


def step_row(source, target, plus, minus, moment, row, tiles, edge):
    def at(field, r, tile):
        return source[field, r, :, pl.ds(tile * LANES, LANES)]

    first_lane, last_lane = edge
    held = {}

    def turned(field, tile):
        tile %= tiles
        if (field, tile) not in held:
            value = at(field, row, tile)
            held[field, tile] = (
                value,
                pltpu.roll(value, 1, 1),
                pltpu.roll(value, LANES - 1, 1),
            )
        return held[field, tile]

    def coefficient(ref, tile, channel):
        line = ref[tile, row - 1, pl.ds(moment * 4 + channel, 1), :]
        return jnp.broadcast_to(line, (8, LANES))

    for tile in range(tiles):
        middle, west, east, south, north = ([], [], [], [], [])
        for field in range(3):
            value, right, left = turned(field, tile)
            middle.append(value)
            west.append(jnp.where(first_lane, turned(field, tile - 1)[1], right))
            east.append(jnp.where(last_lane, turned(field, tile + 1)[2], left))
            south.append(at(field, row - 1, tile))
            north.append(at(field, row + 1, tile))
        to_east = coefficient(plus, tile, 0)
        to_west = coefficient(minus, tile, 0)
        to_north = coefficient(plus, tile, 1)
        to_south = coefficient(minus, tile, 1)
        turn = coefficient(plus, tile, 2)
        depth = coefficient(plus, tile, 3)
        new = [
            (middle[f] + to_east * east[f])
            + (to_west * west[f] + to_north * north[f])
            + to_south * south[f]
            for f in range(3)
        ]
        new[0] = new[0] + depth * ((east[1] - west[1]) + (north[2] - south[2]))
        new[1] = new[1] + (turn * middle[2] - (east[0] - west[0]))
        new[2] = new[2] - (turn * middle[1] + (north[0] - south[0]))
        for field in range(3):
            target(field, row, tile, new[field])


def advance_all(
    place_ref, below_ref, low_ref, high_ref, above_ref, mine_ref, other_hbm, out_ref,
    first, second, plus, minus, other_ref, laid, sem, left
):
    tiles = plus.shape[0]
    rows = out_ref.shape[2]
    half = low_ref.shape[1]
    copies = [
        pltpu.make_async_copy(below_ref, first.at[:, pl.ds(0, HALO)], laid.at[0]),
        pltpu.make_async_copy(above_ref, first.at[:, pl.ds(HALO + rows, HALO)], laid.at[1]),
    ]
    fetches = [
        pltpu.make_async_copy(other_hbm.at[quad, side], other_ref.at[quad, side], sem.at[quad, side])
        for quad in range(tiles // 4)
        for side in range(2)
    ]
    for each in fetches + copies:
        each.start()
    channel = lax.broadcasted_iota(jnp.int32, (8, LANES), 0) % 4
    spread = jnp.where(channel < 2, jnp.float32(SPREAD), jnp.float32(0.0))

    def lay(core, gathered):
        @pl.loop(0, tiles // 4)
        def _(quad):
            for side in range(2):
                tile = quad * 4 + (side ^ place_ref[2]) * 2 + (core ^ place_ref[3])

                def put(row, line, value):
                    lines = pl.ds(line, value.shape[0])
                    plus[tile, row, lines, :] = value + spread[: value.shape[0]]
                    minus[tile, row, lines, :] = SPREAD - value

                for row in range(rows):
                    for pair in range(2):
                        put(3 + row, 8 * pair, gathered[quad, side, 2 * row + pair])
                for start, far, mid, near in ((2 * rows, 0, 1, 2), (2 * rows + 3, 13, 12, 11)):
                    put(mid, 0, gathered[quad, side, start])
                    put(near, 0, gathered[quad, side, start + 1])
                    put(far, 0, gathered[quad, side, start + 2, :4])
                    put(near, 8, gathered[quad, side, start + 2, 4:])

    lay(0, mine_ref)
    for start, ref in ((HALO, low_ref), (HALO + half, high_ref)):

        @pl.loop(0, half)
        def _(row):
            for field in range(3):
                first[field, start + row] = ref[field, row]

    for each in fetches:
        each.wait()
    lay(1, other_ref)

    for each in copies:
        each.wait()
    lane = lax.broadcasted_iota(jnp.int32, (8, LANES), 1)
    edge = (lane == 0, lane == LANES - 1)

    def leaving(field, row):
        return pltpu.make_async_copy(first.at[field, HALO + row], out_ref.at[:, field, row], left.at[field, row])

    @pl.loop(0, STEPS // 2)
    def _(turn):
        for half, (source, goal) in enumerate([(first, second), (second, first)]):
            moment = 2 * turn + half
            begin, end = (moment + 1, rows + 2 * HALO - 1 - moment)
            final = jnp.logical_and(turn == STEPS // 2 - 1, half == 1)
            scales = [jnp.where(final, KEEP**STEPS * (HEIGHT if field == 0 else 1.0), 1.0) for field in range(3)]

            def target(field, row, tile, value):
                if half:
                    value = value * scales[field]
                goal[field, row, :, pl.ds(tile * LANES, LANES)] = value

            @pl.loop(0, (end - begin + BLOCK - 1) // BLOCK)
            def _(block):
                start = jnp.minimum(begin + block * BLOCK, end - BLOCK)
                for row in range(BLOCK):
                    row += start
                    step_row(source, target, plus, minus, moment, row, tiles, edge)
                if half:

                    @pl.when(final)
                    def _():
                        for row in range(BLOCK):
                            for field in range(3):
                                leaving(field, start + row - HALO).start()

            for grid_edge, row in ((0, HALO - 1), (place_ref[1] - 1, HALO + rows)):

                @pl.when(place_ref[0] == grid_edge)
                def _():
                    goal[:, row] = jnp.zeros_like(goal[:, row])

    @pl.loop(0, rows)
    def _(row):
        for field in range(3):
            leaving(field, row).wait()


def shards(perturbation, wind_coriolis, depth_field):
    vectors, fields, rows, lon = perturbation.shape
    tiles = lon // LANES
    count = lax.axis_size("lat")
    up = [(i, i + 1) for i in range(count - 1)]
    down = [(i + 1, i) for i in range(count - 1)]

    low, high = rows_first(perturbation)
    below = lax.ppermute(high, "lat", up)
    above = lax.ppermute(low, "lat", down)

    few = jax.ShapeDtypeStruct((3, 8, LANES), jnp.float32)
    own, to_up, to_down = pl.pallas_call(
        pack,
        out_shape=(jax.ShapeDtypeStruct((2 * rows, 8, LANES), jnp.float32), few, few),
        in_specs=[VMEM] * 2,
        out_specs=(VMEM,) * 3,
        compiler_params=room(4),
    )(wind_coriolis, depth_field)
    own = jnp.concatenate([own, lax.ppermute(to_up, "lat", up), lax.ppermute(to_down, "lat", down)])
    own, low, high = lax.optimization_barrier((own, low, high))
    swap = [(0, 1), (1, 0)]
    mine = jnp.stack([own, lax.ppermute(own, "zh", swap)])
    mine = lax.all_gather(mine, "x", axis=0)
    other = lax.ppermute(mine, "core", swap)

    place = [lax.axis_index("lat"), count, lax.axis_index("zh"), lax.axis_index("core")]
    place = jnp.stack([jnp.int32(number) for number in place])
    table = pltpu.VMEM((tiles, rows + 6, STEPS * 4, LANES), jnp.float32)
    return pl.pallas_call(
        advance_all,
        out_shape=jax.ShapeDtypeStruct(perturbation.shape, perturbation.dtype),
        in_specs=[SMEM, HBM, VMEM, VMEM, HBM, VMEM, HBM],
        out_specs=HBM,
        scratch_shapes=[
            pltpu.VMEM((fields, rows + 2 * HALO, vectors, lon), jnp.float32),
            pltpu.VMEM((fields, rows + 2 * HALO, vectors, lon), jnp.float32),
            table,
            table,
            pltpu.VMEM(other.shape, jnp.float32),
            pltpu.SemaphoreType.DMA((2,)),
            pltpu.SemaphoreType.DMA((tiles // 4, 2)),
            pltpu.SemaphoreType.DMA((fields, rows)),
        ],
        compiler_params=room(14),
    )(place, below, low, high, above, mine, other)


def solution(mesh):
    grid = Mesh(
        mesh.devices.reshape(mesh.shape["vec"] // 4, 2, 2, mesh.shape["lat"]), ("x", "zh", "core", "lat")
    )
    vec = ("x", "zh", "core")
    placed = (P(vec, None, "lat", None), P(None, None, "lat", vec), P(None, "lat", vec))
    return jax.shard_map(
        shards, mesh=grid, in_specs=placed, out_specs=P(vec, None, "lat", None), check_vma=False
    )
```

```python
import jax
import jax.numpy as jnp
from jax import lax
from jax.experimental import pallas as pl
from jax.experimental.pallas import tpu as pltpu
from jax.sharding import Mesh, PartitionSpec as P

STEPS = 4
HALO = 4
BLOCK = 4
LANES = 128

time_step = 0.2
viscosity = 0.05

KEEP = 1.0 - 4.0 * time_step * viscosity
SPREAD = time_step * viscosity / KEEP
SLOPE = time_step / (2.0 * KEEP)
HEIGHT = 2.0 * KEEP / time_step

VMEM = pl.BlockSpec(memory_space=pltpu.VMEM)
HBM = pl.BlockSpec(memory_space=pl.ANY)
SMEM = pl.BlockSpec(memory_space=pltpu.SMEM)


def room(mebibytes):
    return pltpu.CompilerParams(vmem_limit_bytes=mebibytes << 20)


def split_rows(state_ref, low_ref, high_ref):
    fields, rows, lon = state_ref.shape[1:]
    half = rows // 2

    for field in range(fields):

        @pl.loop(0, lon // LANES)
        def _(tile):
            lanes = pl.ds(pl.multiple_of(tile * LANES, LANES), LANES)
            block = jnp.swapaxes(state_ref[:, field, :, lanes], 0, 1)
            if field == 0:
                block = block * (1.0 / HEIGHT)
            low_ref[field, :, :, lanes] = block[:half]
            high_ref[field, :, :, lanes] = block[half:]


def rows_first(state):
    vectors, fields, rows, lon = state.shape
    half = jax.ShapeDtypeStruct((fields, rows // 2, vectors, lon), state.dtype)
    return pl.pallas_call(
        split_rows,
        out_shape=(half, half),
        in_specs=[VMEM],
        out_specs=(VMEM, VMEM),
        compiler_params=room(8),
    )(state)


def pack(wind_hbm, depth_hbm, own_ref, up_ref, down_ref, wind_ref, depth_ref, sems):
    copies = [
        pltpu.make_async_copy(wind_hbm, wind_ref, sems.at[0]),
        pltpu.make_async_copy(depth_hbm, depth_ref, sems.at[1]),
    ]
    for copy in copies:
        copy.start()
    for copy in copies:
        copy.wait()
    for pair in range(STEPS // 2):
        planes = []
        for moment in (2 * pair, 2 * pair + 1):
            planes += [wind_ref[moment, 0] * -SLOPE, wind_ref[moment, 1] * -SLOPE]
            planes += [wind_ref[moment, 2] * (2.0 * SLOPE), depth_ref[moment] * (-SLOPE * SLOPE)]
        block = jnp.swapaxes(jnp.stack(planes), 0, 1)
        for row in range(block.shape[0]):
            own_ref[2 * row + pair] = block[row]
        for out, far, mid, near in ((up_ref, 5, 6, 7), (down_ref, 2, 1, 0)):
            if pair == 0:
                out[0] = block[mid]
                out[1] = block[near]
                out[2, :4] = block[far, :4]
            else:
                out[2, 4:] = block[near, :4]


def step_row(source, target, plus, minus, moment, row, tiles, edge):
    def at(field, r, tile):
        return source[field, r, :, pl.ds(tile * LANES, LANES)]

    first_lane, last_lane = edge
    held = {}

    def turned(field, tile):
        tile %= tiles
        if (field, tile) not in held:
            value = at(field, row, tile)
            held[field, tile] = (
                value,
                pltpu.roll(value, 1, 1),
                pltpu.roll(value, LANES - 1, 1),
            )
        return held[field, tile]

    def coefficient(ref, tile, channel):
        line = ref[tile, row - 1, pl.ds(moment * 4 + channel, 1), :]
        return jnp.broadcast_to(line, (8, LANES))

    for tile in range(tiles):
        middle, west, east, south, north = ([], [], [], [], [])
        for field in range(3):
            value, right, left = turned(field, tile)
            middle.append(value)
            west.append(jnp.where(first_lane, turned(field, tile - 1)[1], right))
            east.append(jnp.where(last_lane, turned(field, tile + 1)[2], left))
            south.append(at(field, row - 1, tile))
            north.append(at(field, row + 1, tile))
        to_east = coefficient(plus, tile, 0)
        to_west = coefficient(minus, tile, 0)
        to_north = coefficient(plus, tile, 1)
        to_south = coefficient(minus, tile, 1)
        turn = coefficient(plus, tile, 2)
        depth = coefficient(plus, tile, 3)
        new = [
            (middle[f] + to_east * east[f])
            + (to_west * west[f] + to_north * north[f])
            + to_south * south[f]
            for f in range(3)
        ]
        new[0] = new[0] + depth * ((east[1] - west[1]) + (north[2] - south[2]))
        new[1] = new[1] + (turn * middle[2] - (east[0] - west[0]))
        new[2] = new[2] - (turn * middle[1] + (north[0] - south[0]))
        for field in range(3):
            target(field, row, tile, new[field])


def advance_all(
    place_ref, below_ref, low_ref, high_ref, above_ref, mine_ref, other_hbm, out_ref,
    first, second, plus, minus, other_ref, laid, sem, left
):
    tiles = plus.shape[0]
    rows = out_ref.shape[2]
    half = low_ref.shape[1]
    copies = [
        pltpu.make_async_copy(below_ref, first.at[:, pl.ds(0, HALO)], laid.at[0]),
        pltpu.make_async_copy(above_ref, first.at[:, pl.ds(HALO + rows, HALO)], laid.at[1]),
    ]
    fetches = [
        pltpu.make_async_copy(other_hbm.at[quad, side], other_ref.at[quad, side], sem.at[quad, side])
        for quad in range(tiles // 4)
        for side in range(2)
    ]
    for each in fetches + copies:
        each.start()
    channel = lax.broadcasted_iota(jnp.int32, (8, LANES), 0) % 4
    spread = jnp.where(channel < 2, jnp.float32(SPREAD), jnp.float32(0.0))

    def lay(core, gathered):
        @pl.loop(0, tiles // 4)
        def _(quad):
            for side in range(2):
                tile = quad * 4 + (side ^ place_ref[2]) * 2 + (core ^ place_ref[3])

                def put(row, line, value):
                    lines = pl.ds(line, value.shape[0])
                    plus[tile, row, lines, :] = value + spread[: value.shape[0]]
                    minus[tile, row, lines, :] = SPREAD - value

                for row in range(rows):
                    for pair in range(2):
                        put(3 + row, 8 * pair, gathered[quad, side, 2 * row + pair])
                for start, far, mid, near in ((2 * rows, 0, 1, 2), (2 * rows + 3, 13, 12, 11)):
                    put(mid, 0, gathered[quad, side, start])
                    put(near, 0, gathered[quad, side, start + 1])
                    put(far, 0, gathered[quad, side, start + 2, :4])
                    put(near, 8, gathered[quad, side, start + 2, 4:])

    lay(0, mine_ref)
    for start, ref in ((HALO, low_ref), (HALO + half, high_ref)):

        @pl.loop(0, half)
        def _(row):
            for field in range(3):
                first[field, start + row] = ref[field, row]

    for each in fetches:
        each.wait()
    lay(1, other_ref)

    for each in copies:
        each.wait()
    lane = lax.broadcasted_iota(jnp.int32, (8, LANES), 1)
    edge = (lane == 0, lane == LANES - 1)

    def leaving(field, row):
        return pltpu.make_async_copy(first.at[field, HALO + row], out_ref.at[:, field, row], left.at[field, row])

    @pl.loop(0, STEPS // 2)
    def _(turn):
        for half, (source, goal) in enumerate([(first, second), (second, first)]):
            moment = 2 * turn + half
            begin, end = (moment + 1, rows + 2 * HALO - 1 - moment)
            final = jnp.logical_and(turn == STEPS // 2 - 1, half == 1)
            scales = [jnp.where(final, KEEP**STEPS * (HEIGHT if field == 0 else 1.0), 1.0) for field in range(3)]

            def target(field, row, tile, value):
                if half:
                    value = value * scales[field]
                goal[field, row, :, pl.ds(tile * LANES, LANES)] = value

            @pl.loop(0, (end - begin + BLOCK - 1) // BLOCK)
            def _(block):
                start = jnp.minimum(begin + block * BLOCK, end - BLOCK)
                for row in range(BLOCK):
                    row += start
                    step_row(source, target, plus, minus, moment, row, tiles, edge)
                if half:

                    @pl.when(final)
                    def _():
                        for row in range(BLOCK):
                            for field in range(3):
                                leaving(field, start + row - HALO).start()

            for grid_edge, row in ((0, HALO - 1), (place_ref[1] - 1, HALO + rows)):

                @pl.when(place_ref[0] == grid_edge)
                def _():
                    goal[:, row] = jnp.zeros_like(goal[:, row])

    @pl.loop(0, rows)
    def _(row):
        for field in range(3):
            leaving(field, row).wait()


def shards(perturbation, wind_coriolis, depth_field):
    vectors, fields, rows, lon = perturbation.shape
    tiles = lon // LANES
    count = lax.axis_size("lat")
    up = [(i, i + 1) for i in range(count - 1)]
    down = [(i + 1, i) for i in range(count - 1)]

    low, high = rows_first(perturbation)
    below = lax.ppermute(high, "lat", up)
    above = lax.ppermute(low, "lat", down)

    few = jax.ShapeDtypeStruct((3, 8, LANES), jnp.float32)
    own, to_up, to_down = pl.pallas_call(
        pack,
        out_shape=(jax.ShapeDtypeStruct((2 * rows, 8, LANES), jnp.float32), few, few),
        in_specs=[pl.BlockSpec(memory_space=pltpu.HBM)] * 2,
        out_specs=(VMEM,) * 3,
        scratch_shapes=[
            pltpu.VMEM(wind_coriolis.shape, jnp.float32),
            pltpu.VMEM(depth_field.shape, jnp.float32),
            pltpu.SemaphoreType.DMA((2,)),
        ],
        compiler_params=room(2),
    )(*(pltpu.with_memory_space_constraint(part, pltpu.HBM) for part in (wind_coriolis, depth_field)))
    own = jnp.concatenate([own, lax.ppermute(to_up, "lat", up), lax.ppermute(to_down, "lat", down)])
    own, low, high = lax.optimization_barrier((own, low, high))
    swap = [(0, 1), (1, 0)]
    mine = jnp.stack([own, lax.ppermute(own, "zh", swap)])
    mine = lax.all_gather(mine, "x", axis=0)
    other = lax.ppermute(mine, "core", swap)

    place = [lax.axis_index("lat"), count, lax.axis_index("zh"), lax.axis_index("core")]
    place = jnp.stack([jnp.int32(number) for number in place])
    table = pltpu.VMEM((tiles, rows + 6, STEPS * 4, LANES), jnp.float32)
    return pl.pallas_call(
        advance_all,
        out_shape=jax.ShapeDtypeStruct(perturbation.shape, perturbation.dtype),
        in_specs=[SMEM, HBM, VMEM, VMEM, HBM, VMEM, HBM],
        out_specs=HBM,
        scratch_shapes=[
            pltpu.VMEM((fields, rows + 2 * HALO, vectors, lon), jnp.float32),
            pltpu.VMEM((fields, rows + 2 * HALO, vectors, lon), jnp.float32),
            table,
            table,
            pltpu.VMEM(other.shape, jnp.float32),
            pltpu.SemaphoreType.DMA((2,)),
            pltpu.SemaphoreType.DMA((tiles // 4, 2)),
            pltpu.SemaphoreType.DMA((fields, rows)),
        ],
        compiler_params=room(14),
    )(place, below, low, high, above, mine, other)


def solution(mesh):
    grid = Mesh(
        mesh.devices.reshape(mesh.shape["vec"] // 4, 2, 2, mesh.shape["lat"]), ("x", "zh", "core", "lat")
    )
    vec = ("x", "zh", "core")
    placed = (P(vec, None, "lat", None), P(None, None, "lat", vec), P(None, "lat", vec))
    return jax.shard_map(
        shards, mesh=grid, in_specs=placed, out_specs=P(vec, None, "lat", None), check_vma=False
    )
```

```python
import jax
import jax.numpy as jnp
from jax import lax
from jax.experimental import pallas as pl
from jax.experimental.pallas import tpu as pltpu
from jax.sharding import Mesh, PartitionSpec as P

STEPS = 4
HALO = 4
BLOCK = 4
LANES = 128

time_step = 0.2
viscosity = 0.05

KEEP = 1.0 - 4.0 * time_step * viscosity
SPREAD = time_step * viscosity / KEEP
SLOPE = time_step / (2.0 * KEEP)
HEIGHT = 2.0 * KEEP / time_step

VMEM = pl.BlockSpec(memory_space=pltpu.VMEM)
HBM = pl.BlockSpec(memory_space=pl.ANY)
SMEM = pl.BlockSpec(memory_space=pltpu.SMEM)


def room(mebibytes):
    return pltpu.CompilerParams(vmem_limit_bytes=mebibytes << 20)


def split_rows(state_hbm, low_ref, high_ref, state_ref, sems):
    fields, rows, lon = state_ref.shape[1:]
    half = rows // 2
    copies = [
        pltpu.make_async_copy(state_hbm.at[:, field], state_ref.at[:, field], sems.at[field])
        for field in range(fields)
    ]
    for copy in copies:
        copy.start()

    for field in range(fields):
        copies[field].wait()

        @pl.loop(0, lon // LANES)
        def _(tile):
            lanes = pl.ds(pl.multiple_of(tile * LANES, LANES), LANES)
            block = jnp.swapaxes(state_ref[:, field, :, lanes], 0, 1)
            if field == 0:
                block = block * (1.0 / HEIGHT)
            low_ref[field, :, :, lanes] = block[:half]
            high_ref[field, :, :, lanes] = block[half:]


def rows_first(state):
    vectors, fields, rows, lon = state.shape
    half = jax.ShapeDtypeStruct((fields, rows // 2, vectors, lon), state.dtype)
    return pl.pallas_call(
        split_rows,
        out_shape=(half, half),
        in_specs=[pl.BlockSpec(memory_space=pltpu.HBM)],
        out_specs=(VMEM, VMEM),
        scratch_shapes=[pltpu.VMEM(state.shape, state.dtype), pltpu.SemaphoreType.DMA((fields,))],
        compiler_params=room(4),
    )(pltpu.with_memory_space_constraint(state, pltpu.HBM))


def pack(wind_hbm, depth_hbm, own_ref, up_ref, down_ref, wind_ref, depth_ref, sems):
    copies = [
        pltpu.make_async_copy(wind_hbm, wind_ref, sems.at[0]),
        pltpu.make_async_copy(depth_hbm, depth_ref, sems.at[1]),
    ]
    for copy in copies:
        copy.start()
    for copy in copies:
        copy.wait()
    for pair in range(STEPS // 2):
        planes = []
        for moment in (2 * pair, 2 * pair + 1):
            planes += [wind_ref[moment, 0] * -SLOPE, wind_ref[moment, 1] * -SLOPE]
            planes += [wind_ref[moment, 2] * (2.0 * SLOPE), depth_ref[moment] * (-SLOPE * SLOPE)]
        block = jnp.swapaxes(jnp.stack(planes), 0, 1)
        for row in range(block.shape[0]):
            own_ref[2 * row + pair] = block[row]
        for out, far, mid, near in ((up_ref, 5, 6, 7), (down_ref, 2, 1, 0)):
            if pair == 0:
                out[0] = block[mid]
                out[1] = block[near]
                out[2, :4] = block[far, :4]
            else:
                out[2, 4:] = block[near, :4]


def step_row(source, target, plus, minus, moment, row, tiles, edge):
    def at(field, r, tile):
        return source[field, r, :, pl.ds(tile * LANES, LANES)]

    first_lane, last_lane = edge
    held = {}

    def turned(field, tile):
        tile %= tiles
        if (field, tile) not in held:
            value = at(field, row, tile)
            held[field, tile] = (
                value,
                pltpu.roll(value, 1, 1),
                pltpu.roll(value, LANES - 1, 1),
            )
        return held[field, tile]

    def coefficient(ref, tile, channel):
        line = ref[tile, row - 1, pl.ds(moment * 4 + channel, 1), :]
        return jnp.broadcast_to(line, (8, LANES))

    for tile in range(tiles):
        middle, west, east, south, north = ([], [], [], [], [])
        for field in range(3):
            value, right, left = turned(field, tile)
            middle.append(value)
            west.append(jnp.where(first_lane, turned(field, tile - 1)[1], right))
            east.append(jnp.where(last_lane, turned(field, tile + 1)[2], left))
            south.append(at(field, row - 1, tile))
            north.append(at(field, row + 1, tile))
        to_east = coefficient(plus, tile, 0)
        to_west = coefficient(minus, tile, 0)
        to_north = coefficient(plus, tile, 1)
        to_south = coefficient(minus, tile, 1)
        turn = coefficient(plus, tile, 2)
        depth = coefficient(plus, tile, 3)
        new = [
            (middle[f] + to_east * east[f])
            + (to_west * west[f] + to_north * north[f])
            + to_south * south[f]
            for f in range(3)
        ]
        new[0] = new[0] + depth * ((east[1] - west[1]) + (north[2] - south[2]))
        new[1] = new[1] + (turn * middle[2] - (east[0] - west[0]))
        new[2] = new[2] - (turn * middle[1] + (north[0] - south[0]))
        for field in range(3):
            target(field, row, tile, new[field])


def advance_all(
    place_ref, below_ref, low_ref, high_ref, above_ref, mine_ref, other_hbm, out_ref,
    first, second, plus, minus, other_ref, laid, sem, left
):
    tiles = plus.shape[0]
    rows = out_ref.shape[2]
    half = low_ref.shape[1]
    copies = [
        pltpu.make_async_copy(below_ref, first.at[:, pl.ds(0, HALO)], laid.at[0]),
        pltpu.make_async_copy(above_ref, first.at[:, pl.ds(HALO + rows, HALO)], laid.at[1]),
    ]
    fetches = [
        pltpu.make_async_copy(other_hbm.at[quad, side], other_ref.at[quad, side], sem.at[quad, side])
        for quad in range(tiles // 4)
        for side in range(2)
    ]
    for each in fetches + copies:
        each.start()
    channel = lax.broadcasted_iota(jnp.int32, (8, LANES), 0) % 4
    spread = jnp.where(channel < 2, jnp.float32(SPREAD), jnp.float32(0.0))

    def lay(core, gathered):
        @pl.loop(0, tiles // 4)
        def _(quad):
            for side in range(2):
                tile = quad * 4 + (side ^ place_ref[2]) * 2 + (core ^ place_ref[3])

                def put(row, line, value):
                    lines = pl.ds(line, value.shape[0])
                    plus[tile, row, lines, :] = value + spread[: value.shape[0]]
                    minus[tile, row, lines, :] = SPREAD - value

                for row in range(rows):
                    for pair in range(2):
                        put(3 + row, 8 * pair, gathered[quad, side, 2 * row + pair])
                for start, far, mid, near in ((2 * rows, 0, 1, 2), (2 * rows + 3, 13, 12, 11)):
                    put(mid, 0, gathered[quad, side, start])
                    put(near, 0, gathered[quad, side, start + 1])
                    put(far, 0, gathered[quad, side, start + 2, :4])
                    put(near, 8, gathered[quad, side, start + 2, 4:])

    lay(0, mine_ref)
    for start, ref in ((HALO, low_ref), (HALO + half, high_ref)):

        @pl.loop(0, half)
        def _(row):
            for field in range(3):
                first[field, start + row] = ref[field, row]

    for each in fetches:
        each.wait()
    lay(1, other_ref)

    for each in copies:
        each.wait()
    lane = lax.broadcasted_iota(jnp.int32, (8, LANES), 1)
    edge = (lane == 0, lane == LANES - 1)

    def leaving(field, row):
        return pltpu.make_async_copy(first.at[field, HALO + row], out_ref.at[:, field, row], left.at[field, row])

    @pl.loop(0, STEPS // 2)
    def _(turn):
        for half, (source, goal) in enumerate([(first, second), (second, first)]):
            moment = 2 * turn + half
            begin, end = (moment + 1, rows + 2 * HALO - 1 - moment)
            final = jnp.logical_and(turn == STEPS // 2 - 1, half == 1)
            scales = [jnp.where(final, KEEP**STEPS * (HEIGHT if field == 0 else 1.0), 1.0) for field in range(3)]

            def target(field, row, tile, value):
                if half:
                    value = value * scales[field]
                goal[field, row, :, pl.ds(tile * LANES, LANES)] = value

            @pl.loop(0, (end - begin + BLOCK - 1) // BLOCK)
            def _(block):
                start = jnp.minimum(begin + block * BLOCK, end - BLOCK)
                for row in range(BLOCK):
                    row += start
                    step_row(source, target, plus, minus, moment, row, tiles, edge)
                if half:

                    @pl.when(final)
                    def _():
                        for row in range(BLOCK):
                            for field in range(3):
                                leaving(field, start + row - HALO).start()

            for grid_edge, row in ((0, HALO - 1), (place_ref[1] - 1, HALO + rows)):

                @pl.when(place_ref[0] == grid_edge)
                def _():
                    goal[:, row] = jnp.zeros_like(goal[:, row])

    @pl.loop(0, rows)
    def _(row):
        for field in range(3):
            leaving(field, row).wait()


def shards(perturbation, wind_coriolis, depth_field):
    vectors, fields, rows, lon = perturbation.shape
    tiles = lon // LANES
    count = lax.axis_size("lat")
    up = [(i, i + 1) for i in range(count - 1)]
    down = [(i + 1, i) for i in range(count - 1)]

    low, high = rows_first(perturbation)
    below = lax.ppermute(high, "lat", up)
    above = lax.ppermute(low, "lat", down)

    few = jax.ShapeDtypeStruct((3, 8, LANES), jnp.float32)
    own, to_up, to_down = pl.pallas_call(
        pack,
        out_shape=(jax.ShapeDtypeStruct((2 * rows, 8, LANES), jnp.float32), few, few),
        in_specs=[pl.BlockSpec(memory_space=pltpu.HBM)] * 2,
        out_specs=(VMEM,) * 3,
        scratch_shapes=[
            pltpu.VMEM(wind_coriolis.shape, jnp.float32),
            pltpu.VMEM(depth_field.shape, jnp.float32),
            pltpu.SemaphoreType.DMA((2,)),
        ],
        compiler_params=room(2),
    )(*(pltpu.with_memory_space_constraint(part, pltpu.HBM) for part in (wind_coriolis, depth_field)))
    own = jnp.concatenate([own, lax.ppermute(to_up, "lat", up), lax.ppermute(to_down, "lat", down)])
    own, low, high = lax.optimization_barrier((own, low, high))
    swap = [(0, 1), (1, 0)]
    mine = jnp.stack([own, lax.ppermute(own, "zh", swap)])
    mine = lax.all_gather(mine, "x", axis=0)
    other = lax.ppermute(mine, "core", swap)

    place = [lax.axis_index("lat"), count, lax.axis_index("zh"), lax.axis_index("core")]
    place = jnp.stack([jnp.int32(number) for number in place])
    table = pltpu.VMEM((tiles, rows + 6, STEPS * 4, LANES), jnp.float32)
    return pl.pallas_call(
        advance_all,
        out_shape=jax.ShapeDtypeStruct(perturbation.shape, perturbation.dtype),
        in_specs=[SMEM, HBM, VMEM, VMEM, HBM, VMEM, HBM],
        out_specs=HBM,
        scratch_shapes=[
            pltpu.VMEM((fields, rows + 2 * HALO, vectors, lon), jnp.float32),
            pltpu.VMEM((fields, rows + 2 * HALO, vectors, lon), jnp.float32),
            table,
            table,
            pltpu.VMEM(other.shape, jnp.float32),
            pltpu.SemaphoreType.DMA((2,)),
            pltpu.SemaphoreType.DMA((tiles // 4, 2)),
            pltpu.SemaphoreType.DMA((fields, rows)),
        ],
        compiler_params=room(14),
    )(place, below, low, high, above, mine, other)


def solution(mesh):
    grid = Mesh(
        mesh.devices.reshape(mesh.shape["vec"] // 4, 2, 2, mesh.shape["lat"]), ("x", "zh", "core", "lat")
    )
    vec = ("x", "zh", "core")
    placed = (P(vec, None, "lat", None), P(None, None, "lat", vec), P(None, "lat", vec))
    return jax.shard_map(
        shards, mesh=grid, in_specs=placed, out_specs=P(vec, None, "lat", None), check_vma=False
    )
```
